32 devices in a mesh: dp: 16 (over z, x, core), blk: 2 (over y).
Axes of the slice: x: 2, y: 2, z: 4, core: 2. Of those that a mesh axis runs over, the one named last changes fastest.
Arguments:
- tokens: bfloat16 [16, 1024, 768], P('dp', 'blk'), may hold values from -6 to 6
- first_values: bfloat16 [16, 1024, 384], P('dp', 'blk'), may hold values from -6 to 6
- segments: int32 [16, 1024], P('dp', 'blk'), may hold values from 0 to 1023, as said below
- w_query: bfloat16 [768, 768], replicated, may hold values from -0.21875 to 0.21875
- b_query: bfloat16 [768], replicated, may hold values from -2 to 2
- w_key: bfloat16 [768, 768], replicated, may hold values from -0.21875 to 0.21875
- w_value: bfloat16 [768, 384], replicated, may hold values from -0.21875 to 0.21875
- b_value: bfloat16 [384], replicated, may hold values from -3 to 3
- w_out: bfloat16 [768, 768], replicated, may hold values from -1.75 to 1.75
- b_out: bfloat16 [768], replicated, may hold values from -2 to 2
- gain_one: bfloat16 [768], replicated, may hold values from 0.5 to 1.5
- bias_one: bfloat16 [768], replicated, may hold values from -2 to 2
- gain_two: bfloat16 [768], replicated, may hold values from 0.5 to 1.5
- bias_two: bfloat16 [768], replicated, may hold values from -2 to 2
- w_up: bfloat16 [768, 3072], replicated, may hold values from -0.21875 to 0.21875
- b_up: bfloat16 [3072], replicated, may hold values from -3 to 3
- w_down: bfloat16 [3072, 768], replicated, may hold values from -0.109375 to 0.109375
- b_down: bfloat16 [768], replicated, may hold values from -2 to 2
- cotangent: bfloat16 [16, 1024, 768], P('dp', 'blk'), may hold values from -6 to 6
Outputs:
- output: bfloat16 [16, 1024, 768], P('dp', 'blk')
- grad_tokens: float32 [16, 1024, 768], P('dp', 'blk')
- grad_first_values: float32 [16, 1024, 384], P('dp', 'blk')
- grad_w_query: float32 [768, 768], replicated
- grad_b_query: float32 [768], replicated
- grad_w_key: float32 [768, 768], replicated
- grad_w_value: float32 [768, 384], replicated
- grad_b_value: float32 [384], replicated
- grad_w_out: float32 [768, 768], replicated
- grad_b_out: float32 [768], replicated
- grad_gain_one: float32 [768], replicated
- grad_bias_one: float32 [768], replicated
- grad_gain_two: float32 [768], replicated
- grad_bias_two: float32 [768], replicated
- grad_w_up: float32 [768, 3072], replicated
- grad_b_up: float32 [3072], replicated
- grad_w_down: float32 [3072, 768], replicated
- grad_b_down: float32 [768], replicated
The draws below stay inside these ranges and needn't reach their ends.
Inputs may be any that keep to these rules, and one draw needn't show every extreme that they name: `segments`: each token's number is the position within its sequence of the first token of its document, so numbers never fall; the last token of every sequence begins a document of its own; in every sequence one document begins within its first 512 tokens and ends within its last 512.
All inputs are finite; a program needn't handle non-finite values.
Results may differ from the reference program's by a relative error of at most 0.025.
Values may be sent and summed in bfloat16 or wider, within the bound.
No kernel may reach another device: no remote copies, remote signals or barrier semaphores. Data moves between devices by JAX's collectives and lax.ppermute only.
A program may use at most 192 MiB of HBM per device.

```python
import jax
import jax.numpy as jnp
from jax import lax

D = 768
HEADS = 12
HD = 64
FRESH = 6
FF = 3072
LENGTH = 1024
BLOCK = 512
SEQS = 16


def draw_segments(key, part):
    key = jax.random.fold_in(key, 11)
    first_key, last_key, mark_key = jax.random.split(key, 3)
    first = jax.random.randint(first_key, (SEQS, 1), 1, BLOCK)
    last = jax.random.randint(last_key, (SEQS, 1), LENGTH - BLOCK + 1, LENGTH - 1)
    marks = jax.random.randint(mark_key, (SEQS, LENGTH), 0, 48) == 0
    places = jnp.arange(LENGTH, dtype=jnp.int32)[None, :]
    inside = (places > first) & (places < last)
    bounds = (jnp.where(inside, False, marks) | (places == first) | (places == last) | (places == LENGTH - 1)) & (places > 0)
    starts = jnp.where(bounds, places, jnp.zeros_like(places)).astype(jnp.int32)
    numbers = lax.cummax(starts, axis=1)
    return numbers.astype(jnp.int32)


def block_scale(key, extent, cuts, smallest, largest):
    gain, own = 1.0, jax.random.fold_in(key, 6)
    for axis_at, parts in cuts:
        heights = jnp.exp(jax.random.uniform(jax.random.fold_in(own, axis_at), (parts,), jnp.float32, smallest / len(cuts), largest / len(cuts)))
        gain = gain * jnp.repeat(heights, extent[axis_at] // parts).reshape([-1 if axis == axis_at else 1 for axis in range(len(extent))])
    return gain


def gaussian(rng, extent, width, bound, shards=(), held_as=jnp.bfloat16):
    values = jax.random.normal(rng, extent, jnp.float32) * width
    if len(shards) > 0:
        values = block_scale(rng, extent, shards, -0.22, 0.18) * values
    return jnp.clip(values, min=-bound, max=bound).astype(held_as)


def setup_inputs(seed: int = 0) -> dict:
    arg_keys = jax.random.split(jax.random.key(seed), 20)
    return {
        "tokens": gaussian(arg_keys[0], (SEQS, LENGTH, D), 1.0, 6.0, ((0, 16), (1, 2))),
        "first_values": gaussian(arg_keys[1], (SEQS, LENGTH, FRESH * HD), 1.0, 6.0, ((0, 16), (1, 2))),
        "segments": draw_segments(jax.random.fold_in(arg_keys[19], 71), 0),
        "w_query": gaussian(arg_keys[3], (D, D), D ** -0.5, 0.21875),
        "b_query": gaussian(arg_keys[4], (D,), 0.3, 2.0),
        "w_key": gaussian(arg_keys[5], (D, D), D ** -0.5, 0.21875),
        "w_value": gaussian(arg_keys[6], (D, FRESH * HD), D ** -0.5, 0.21875),
        "b_value": gaussian(arg_keys[7], (FRESH * HD,), 0.5, 3.0),
        "w_out": gaussian(arg_keys[8], (D, D), (D // 64) ** -0.5, 1.75),
        "b_out": gaussian(arg_keys[9], (D,), 0.3, 2.0),
        "gain_one": jnp.clip(1.0 + 0.1 * jax.random.normal(arg_keys[10], (D,), jnp.float32), 0.5, 1.5).astype(jnp.bfloat16),
        "bias_one": gaussian(arg_keys[11], (D,), 0.3, 2.0),
        "gain_two": jnp.clip(1.0 + 0.1 * jax.random.normal(arg_keys[12], (D,), jnp.float32), 0.5, 1.5).astype(jnp.bfloat16),
        "bias_two": gaussian(arg_keys[13], (D,), 0.3, 2.0),
        "w_up": gaussian(arg_keys[14], (D, FF), D ** -0.5, 0.21875),
        "b_up": gaussian(arg_keys[15], (FF,), 0.5, 3.0),
        "w_down": gaussian(arg_keys[16], (FF, D), FF ** -0.5, 0.109375),
        "b_down": gaussian(arg_keys[17], (D,), 0.3, 2.0),
        "cotangent": gaussian(arg_keys[18], (SEQS, LENGTH, D), 1.0, 6.0, ((0, 16), (1, 2))),
    }


@jax.custom_vjp
def low(v):
    return lax.optimization_barrier(v.astype(jnp.bfloat16)).astype(jnp.float32)

@jax.custom_vjp
def low_back(v):
    return v

def low_keep(v):
    return (low(v), None)

def low_pass(kept, grad):
    return (grad,)

def back_keep(v):
    return (v, None)

def back_low(kept, grad):
    return (low(grad),)
low.defvjp(low_keep, low_pass)
low_back.defvjp(back_keep, back_low)
epsilon = 1e-05
precise = lax.Precision.HIGHEST
masked_score = -1e+30

def layer_norm(values, gain_vec, bias_vec):
    centered = values - lax.optimization_barrier(jnp.mean(values, axis=-1, keepdims=True))
    spread = lax.optimization_barrier(jnp.mean(centered * centered, axis=-1, keepdims=True))
    return centered * lax.rsqrt(spread + epsilon) * gain_vec + bias_vec

def both_ways(values):
    return low(low_back(values))

def product(left, right):
    return jnp.dot(left, right, precision=precise)

def attend_one(queries, key_proj, all_values, seg_ids):
    places = jnp.arange(queries.shape[0], dtype=jnp.int32)
    scores = jnp.einsum('qhd,khd->hqk', queries, key_proj, precision=precise) * HD ** (-0.5)
    scores = low_back(scores)
    visible = (places[None, :] <= places[:, None]) & (seg_ids[None, :] == seg_ids[:, None])
    scores = jnp.where(visible[None], scores, masked_score)
    row_max = lax.optimization_barrier(jnp.max(scores, axis=-1, keepdims=True))
    weights = jnp.where(visible[None], jnp.exp(scores - row_max), 0.0)
    weights = low(weights / lax.optimization_barrier(jnp.sum(weights, axis=-1, keepdims=True)))
    return jnp.einsum('hqk,khd->qhd', weights, all_values, precision=precise)

def attend_entry(entries):
    queries, key_proj, all_values, seg_ids = entries
    return attend_one(queries, key_proj, all_values, seg_ids)

def forward(tokens, first_values, params, segments):
    w_query, b_query, w_key, w_value, b_value, w_out, b_out, gain_one, bias_one, gain_two, bias_two, w_up, b_up, w_down, b_down = params
    seq_count = tokens.shape[0]
    flat_tokens = tokens.reshape(-1, D)
    flat_first = first_values.reshape(-1, FRESH * HD)
    normed = low(layer_norm(flat_tokens, gain_one, bias_one))
    queries = both_ways(product(normed, w_query) + b_query)
    key_proj = both_ways(product(normed, w_key))
    fresh_vals = both_ways(product(normed, w_value) + b_value)
    all_values = jnp.concatenate([fresh_vals, flat_first], axis=1)
    attended = lax.map(jax.checkpoint(attend_entry), (queries.reshape(seq_count, LENGTH, HEADS, HD), key_proj.reshape(seq_count, LENGTH, HEADS, HD), all_values.reshape(seq_count, LENGTH, HEADS, HD), segments.reshape(seq_count, LENGTH)))
    attn_out = both_ways(attended.reshape(flat_tokens.shape[0], HEADS * HD))
    branch = low_back(product(attn_out, w_out) + b_out)
    middle = flat_tokens + branch
    normed_two = low(layer_norm(middle, gain_two, bias_two))
    hidden = low_back(product(normed_two, w_up) + b_up)
    active = low(jax.nn.gelu(hidden, approximate=True))
    result = middle + product(active, w_down) + b_down
    return result.reshape(seq_count, LENGTH, D)

def reference(tokens, first_values, segments, w_query, b_query, w_key, w_value, b_value, w_out, b_out, gain_one, bias_one, gain_two, bias_two, w_up, b_up, w_down, b_down, cotangent):
    params = tuple((item.astype(jnp.float32) for item in (w_query, b_query, w_key, w_value, b_value, w_out, b_out, gain_one, bias_one, gain_two, bias_two, w_up, b_up, w_down, b_down)))

    def layer_fn(inputs, firsts, weights):
        return forward(inputs, firsts, weights, segments)
    output, pullback = jax.vjp(layer_fn, tokens.astype(jnp.float32), first_values.astype(jnp.float32), params)
    grad_tokens, grad_first, grad_params = pullback(cotangent.astype(jnp.float32))
    g_wq, g_bq, g_wk, g_wv, g_bv, g_wo, g_bo, g_g1, g_b1, g_g2, g_b2, g_wu, g_bu, g_wd, g_bd = grad_params
    return (output.astype(jnp.bfloat16), grad_tokens, grad_first, g_wq, g_bq, g_wk, g_wv, g_bv, g_wo, g_bo, g_g1, g_b1, g_g2, g_b2, g_wu, g_bu, g_wd, g_bd)
```

```python
import functools

import jax
import jax.numpy as jnp
from jax import lax
from jax.sharding import PartitionSpec as P

HEADS = 12
HD = 64


epsilon = 1e-05
masked_score = -1e30


def layer_norm(values, gain_vec, bias_vec):
    centered = values - jnp.mean(values, axis=-1, keepdims=True)
    spread = jnp.mean(centered * centered, axis=-1, keepdims=True)
    return centered * lax.rsqrt(spread + epsilon) * gain_vec + bias_vec


def gelu_tanh(values):
    return jax.nn.gelu(values, approximate=True)


def split_heads(block):
    return block.reshape(block.shape[:-1] + (HEADS, HD))


def unchanged(state):
    return state


def block_scores(query_heads, key_heads, query_place, query_seg, key_place, key_seg):
    scores = jnp.einsum(
        "sqhd,skhd->shqk", query_heads, key_heads, preferred_element_type=jnp.float32
    ) * HD ** (-0.5)
    visible = (key_place[None, None, :] <= query_place[None, :, None]) & (
        key_seg[:, None, :] == query_seg[:, :, None]
    )
    return (scores, visible)


def forward_block(
    carried, key_block, value_block, key_seg, key_start, query_heads, query_place, query_seg
):

    def update(state):
        run_max, run_sum, run_acc = state
        key_place = key_start + jnp.arange(key_block.shape[1], dtype=jnp.int32)
        scores, visible = block_scores(
            query_heads, split_heads(key_block), query_place, query_seg, key_place, key_seg
        )
        scores = jnp.where(visible[:, None], scores, masked_score)
        new_max = jnp.maximum(run_max, jnp.max(scores, axis=-1))
        weights = jnp.where(visible[:, None], jnp.exp(scores - new_max[..., None]), 0.0)
        factor = jnp.exp(run_max - new_max)
        run_sum = run_sum * factor + jnp.sum(weights, axis=-1)
        mixed_in = jnp.einsum(
            "shqk,skhd->sqhd",
            weights.astype(jnp.bfloat16),
            split_heads(value_block),
            preferred_element_type=jnp.float32,
        )
        return (new_max, run_sum, run_acc * jnp.swapaxes(factor, 1, 2)[..., None] + mixed_in)

    return lax.cond(key_start <= query_place[-1], update, unchanged, carried)


def backward_block(
    query_heads,
    grad_heads,
    logsum,
    deltas,
    query_place,
    query_seg,
    key_block,
    value_block,
    key_place,
    key_seg,
):
    key_heads = split_heads(key_block)
    scores, visible = block_scores(
        query_heads, key_heads, query_place, query_seg, key_place, key_seg
    )
    weights = jnp.where(visible[:, None], jnp.exp(scores - logsum[..., None]), 0.0)
    grad_values = jnp.einsum(
        "shqk,sqhd->skhd",
        weights.astype(jnp.bfloat16),
        grad_heads,
        preferred_element_type=jnp.float32,
    )
    grad_weights = jnp.einsum(
        "sqhd,skhd->shqk", grad_heads, split_heads(value_block), preferred_element_type=jnp.float32
    )
    grad_scores = (weights * (grad_weights - deltas[..., None])).astype(jnp.bfloat16)
    grad_query = jnp.einsum(
        "shqk,skhd->sqhd", grad_scores, key_heads, preferred_element_type=jnp.float32
    ) * HD ** (-0.5)
    grad_keys = jnp.einsum(
        "shqk,sqhd->skhd", grad_scores, query_heads, preferred_element_type=jnp.float32
    ) * HD ** (-0.5)
    return (grad_query, grad_keys, grad_values)


LANES = 128


def pairs(count, bit):
    return [(number, number ^ (1 << bit)) for number in range(count)]


def bit_set(axis):
    name, _, bit = axis
    return (lax.axis_index(name) >> bit) & 1


def sum_halves(rows, axis):
    name, count, bit = axis
    half = rows.shape[0] // 2
    mine = bit_set(axis)
    sent = lax.dynamic_slice_in_dim(rows, (1 - mine) * half, half, 0)
    kept = lax.dynamic_slice_in_dim(rows, mine * half, half, 0)
    return kept + lax.ppermute(sent, name, pairs(count, bit))


def join_halves(rows, axis):
    name, count, bit = axis
    other = lax.ppermute(rows, name, pairs(count, bit))
    return jnp.where(
        bit_set(axis) == 0,
        jnp.concatenate([rows, other], 0),
        jnp.concatenate([other, rows], 0),
    )


def sum_everywhere(piece, dp_count, blk_count):
    bits = dp_count.bit_length() - 1
    core, across, *along = [("dp", dp_count, bit) for bit in range(bits)]
    up = [("blk", blk_count, bit) for bit in range(blk_count.bit_length() - 1)]
    orders = ([across, *up], [*up, across])
    rows = sum_halves(piece, core)
    half = rows.shape[0] // 2
    parts = []
    for order, part in zip(orders, (rows[:half], rows[half:])):
        for axis in order:
            part = sum_halves(part, axis)
        parts.append(part)
    share = parts[0].shape[0]
    rows = jnp.concatenate(parts, 0)
    for axis in along:
        rows = sum_halves(rows, axis)
    for axis in reversed(along):
        rows = join_halves(rows, axis)
    parts = []
    for order, part in zip(orders, (rows[:share], rows[share:])):
        for axis in reversed(order):
            part = join_halves(part, axis)
        parts.append(part)
    return join_halves(jnp.concatenate(parts, 0), core).astype(jnp.float32)


def pack_vectors(vectors, rows):
    flat = jnp.concatenate([vector.astype(jnp.bfloat16) for vector in vectors])
    return jnp.pad(flat, (0, rows * LANES - flat.shape[0])).reshape(rows, LANES)


def unpack_vectors(block, lengths):
    flat = block.reshape(-1)
    found, at = [], 0
    for length in lengths:
        found.append(flat[at : at + length])
        at += length
    return found


def body(
    dp_count,
    blk_count,
    tokens,
    first_values,
    segments,
    w_query,
    b_query,
    w_key,
    w_value,
    b_value,
    w_out,
    b_out,
    gain_one,
    bias_one,
    gain_two,
    bias_two,
    w_up,
    b_up,
    w_down,
    b_down,
    cotangent,
):
    seq_here, own_rows, width = tokens.shape
    flat_rows = seq_here * own_rows
    hidden_width = w_up.shape[1]
    query_place = lax.axis_index("blk") * own_rows + jnp.arange(own_rows, dtype=jnp.int32)
    residual_in = tokens.reshape(flat_rows, width).astype(jnp.float32)
    norm_one, pull_one = jax.vjp(
        layer_norm, residual_in, gain_one.astype(jnp.float32), bias_one.astype(jnp.float32)
    )
    normed = norm_one.astype(jnp.bfloat16)
    query_low = (
        jnp.dot(normed, w_query, preferred_element_type=jnp.float32) + b_query.astype(jnp.float32)
    ).astype(jnp.bfloat16)
    key_low = jnp.dot(normed, w_key, preferred_element_type=jnp.float32).astype(jnp.bfloat16)
    fresh_low = (
        jnp.dot(normed, w_value, preferred_element_type=jnp.float32) + b_value.astype(jnp.float32)
    ).astype(jnp.bfloat16)
    fresh_width = fresh_low.shape[1]
    value_low = jnp.concatenate([fresh_low, first_values.reshape(flat_rows, -1)], axis=1)
    query_three = query_low.reshape(seq_here, own_rows, -1)
    key_three = key_low.reshape(seq_here, own_rows, -1)
    value_three = value_low.reshape(seq_here, own_rows, -1)
    query_heads = split_heads(query_three)
    start_state = (
        jnp.full((seq_here, HEADS, own_rows), masked_score, jnp.float32),
        jnp.zeros((seq_here, HEADS, own_rows), jnp.float32),
        jnp.zeros((seq_here, own_rows, HEADS, HD), jnp.float32),
    )
    key_rows = lax.all_gather(key_three, "blk", axis=1, tiled=True)
    value_rows = lax.all_gather(value_three, "blk", axis=1, tiled=True)
    seg_rows = lax.all_gather(segments, "blk", axis=1, tiled=True)
    piece_rows = key_rows.shape[1]
    block_count = piece_rows // own_rows

    def inner(number, state):
        begin = number * own_rows
        key_block = lax.dynamic_slice_in_dim(key_rows, begin, own_rows, 1)
        value_block = lax.dynamic_slice_in_dim(value_rows, begin, own_rows, 1)
        seg_block = lax.dynamic_slice_in_dim(seg_rows, begin, own_rows, 1)
        return forward_block(
            state, key_block, value_block, seg_block, begin, query_heads, query_place, segments
        )

    run_max, run_sum, run_acc = lax.fori_loop(0, block_count, inner, start_state)
    out_heads = run_acc / jnp.swapaxes(run_sum, 1, 2)[..., None]
    logsum = run_max + jnp.log(run_sum)
    out_low = out_heads.reshape(flat_rows, -1).astype(jnp.bfloat16)
    middle = (
        residual_in
        + jnp.dot(out_low, w_out, preferred_element_type=jnp.float32)
        + b_out.astype(jnp.float32)
    )
    norm_two, pull_two = jax.vjp(
        layer_norm, middle, gain_two.astype(jnp.float32), bias_two.astype(jnp.float32)
    )
    normed_two = norm_two.astype(jnp.bfloat16)
    hidden = jnp.dot(normed_two, w_up, preferred_element_type=jnp.float32) + b_up.astype(
        jnp.float32
    )
    active, pull_gelu = jax.vjp(gelu_tanh, hidden)
    active_low = active.astype(jnp.bfloat16)
    output = (
        middle
        + jnp.dot(active_low, w_down, preferred_element_type=jnp.float32)
        + b_down.astype(jnp.float32)
    )
    cot_flat = cotangent.reshape(flat_rows, width)
    grad_out = cot_flat.astype(jnp.float32)
    grad_active = jnp.einsum("td,fd->tf", cot_flat, w_down, preferred_element_type=jnp.float32)
    grad_w_down = jnp.einsum("tf,td->fd", active_low, cot_flat, preferred_element_type=jnp.float32)
    grad_b_down = jnp.sum(grad_out, axis=0)
    (grad_hidden,) = pull_gelu(grad_active)
    hidden_low = grad_hidden.astype(jnp.bfloat16)
    grad_w_up = jnp.einsum("td,tf->df", normed_two, hidden_low, preferred_element_type=jnp.float32)
    grad_b_up = jnp.sum(hidden_low.astype(jnp.float32), axis=0)
    grad_normed_two = jnp.einsum("tf,df->td", hidden_low, w_up, preferred_element_type=jnp.float32)
    grad_middle_part, grad_gain_two, grad_bias_two = pull_two(grad_normed_two)
    grad_middle = grad_out + grad_middle_part
    branch_low = grad_middle.astype(jnp.bfloat16)
    grad_w_out = jnp.einsum("te,td->ed", out_low, branch_low, preferred_element_type=jnp.float32)
    grad_b_out = jnp.sum(branch_low.astype(jnp.float32), axis=0)
    heads_low = jnp.einsum(
        "td,ed->te", branch_low, w_out, preferred_element_type=jnp.float32
    ).astype(jnp.bfloat16)
    heads_three = heads_low.reshape(seq_here, own_rows, -1)
    grad_heads = split_heads(heads_three)
    delta_rows = jnp.sum(grad_heads.astype(jnp.float32) * out_heads, axis=-1)
    deltas = jnp.swapaxes(delta_rows, 1, 2)
    keys_all, values_all, segs_all = (
        lax.all_gather(key_three[None], "blk", axis=0, tiled=True),
        lax.all_gather(value_three[None], "blk", axis=0, tiled=True),
        lax.all_gather(segments[None], "blk", axis=0, tiled=True),
    )
    block_count = keys_all.shape[0]
    gathered = (keys_all, values_all, segs_all, jnp.arange(block_count, dtype=jnp.int32))
    zero_heads = jnp.zeros((seq_here, own_rows, HEADS, HD), jnp.float32)

    def back_step(grad_acc, entries):
        key_block, value_block, seg_block, number = entries
        key_start = number * own_rows
        key_place = key_start + jnp.arange(own_rows, dtype=jnp.int32)

        def compute(acc_in):
            part_q, part_k, part_v = backward_block(
                query_heads,
                grad_heads,
                logsum,
                deltas,
                query_place,
                segments,
                key_block,
                value_block,
                key_place,
                seg_block,
            )
            return (acc_in + part_q, part_k, part_v)

        def skipped(acc_in):
            return (acc_in, zero_heads, zero_heads)

        grad_acc, part_k, part_v = lax.cond(
            key_start <= query_place[-1], compute, skipped, grad_acc
        )
        return (
            grad_acc,
            (part_k.reshape(seq_here, own_rows, -1), part_v.reshape(seq_here, own_rows, -1)),
        )

    grad_query, (terms_k, terms_v) = lax.scan(back_step, zero_heads, gathered)
    grad_key, grad_vals = (
        lax.psum_scatter(
            terms_k.astype(jnp.bfloat16), "blk", scatter_dimension=0, tiled=True
        ).astype(jnp.float32),
        lax.psum_scatter(
            terms_v.astype(jnp.bfloat16), "blk", scatter_dimension=0, tiled=True
        ).astype(jnp.float32),
    )
    grad_key = grad_key.reshape(flat_rows, -1)
    grad_vals = grad_vals.reshape(flat_rows, -1)
    query_grad_low = grad_query.reshape(flat_rows, -1).astype(jnp.bfloat16)
    key_grad_low = grad_key.astype(jnp.bfloat16)
    fresh_grad_low = grad_vals[:, :fresh_width].astype(jnp.bfloat16)
    grad_first = grad_vals[:, fresh_width:]
    grad_w_query = jnp.einsum(
        "td,te->de", normed, query_grad_low, preferred_element_type=jnp.float32
    )
    grad_b_query = jnp.sum(query_grad_low.astype(jnp.float32), axis=0)
    grad_w_key = jnp.einsum("td,te->de", normed, key_grad_low, preferred_element_type=jnp.float32)
    grad_w_value = jnp.einsum(
        "td,te->de", normed, fresh_grad_low, preferred_element_type=jnp.float32
    )
    grad_b_value = jnp.sum(fresh_grad_low.astype(jnp.float32), axis=0)
    grad_normed = (
        jnp.einsum("te,de->td", query_grad_low, w_query, preferred_element_type=jnp.float32)
        + jnp.einsum("te,de->td", key_grad_low, w_key, preferred_element_type=jnp.float32)
        + jnp.einsum("te,de->td", fresh_grad_low, w_value, preferred_element_type=jnp.float32)
    )
    grad_input_part, grad_gain_one, grad_bias_one = pull_one(grad_normed)
    grad_tokens = grad_middle + grad_input_part
    pieces = (
        grad_w_down.astype(jnp.bfloat16),
        grad_w_up.astype(jnp.bfloat16),
        jnp.concatenate(
            [
                grad_w_out.astype(jnp.bfloat16),
                grad_w_query.astype(jnp.bfloat16),
                grad_w_key.astype(jnp.bfloat16),
                grad_w_value.astype(jnp.bfloat16),
                pack_vectors(
                    (
                        grad_b_query,
                        grad_b_value,
                        grad_b_out,
                        grad_gain_one,
                        grad_bias_one,
                        grad_gain_two,
                        grad_bias_two,
                        grad_b_up,
                        grad_b_down,
                    ),
                    width,
                ),
            ],
            axis=1,
        ),
    )
    sum_down, sum_up, rest = [sum_everywhere(piece, dp_count, blk_count) for piece in pieces]
    sum_out, sum_query, sum_key, sum_value, sum_vec = jnp.split(
        rest, [width, 2 * width, 3 * width, 3 * width + fresh_width], axis=1
    )
    (
        vec_query,
        vec_value,
        vec_out,
        vec_gain_one,
        vec_bias_one,
        vec_gain_two,
        vec_bias_two,
        vec_up,
        vec_down,
    ) = unpack_vectors(
        sum_vec, (width, fresh_width, width, width, width, width, width, hidden_width, width)
    )
    totals = (
        sum_query,
        vec_query,
        sum_key,
        sum_value,
        vec_value,
        sum_out,
        vec_out,
        vec_gain_one,
        vec_bias_one,
        vec_gain_two,
        vec_bias_two,
        sum_up,
        vec_up,
        sum_down,
        vec_down,
    )
    return (
        output.reshape(seq_here, own_rows, width).astype(jnp.bfloat16),
        grad_tokens.reshape(seq_here, own_rows, width),
        grad_first.reshape(seq_here, own_rows, -1),
        totals[0],
        totals[1],
        totals[2],
        totals[3],
        totals[4],
        totals[5],
        totals[6],
        totals[7],
        totals[8],
        totals[9],
        totals[10],
        totals[11],
        totals[12],
        totals[13],
        totals[14],
    )


def solution(mesh):
    in_specs = (
        P("dp", "blk", None),
        P("dp", "blk", None),
        P("dp", "blk"),
        P(),
        P(),
        P(),
        P(),
        P(),
        P(),
        P(),
        P(),
        P(),
        P(),
        P(),
        P(),
        P(),
        P(),
        P(),
        P("dp", "blk", None),
    )
    out_specs = (
        P("dp", "blk", None),
        P("dp", "blk", None),
        P("dp", "blk", None),
        P(),
        P(),
        P(),
        P(),
        P(),
        P(),
        P(),
        P(),
        P(),
        P(),
        P(),
        P(),
        P(),
        P(),
        P(),
    )
    placed = functools.partial(body, mesh.shape["dp"], mesh.shape["blk"])
    return jax.shard_map(placed, mesh=mesh, in_specs=in_specs, out_specs=out_specs, check_vma=False)
```
